768 devices in a mesh: ctx: 24 (over z_lo, x), tp: 32 (over z_hi, y, core).
Axes of the slice: x: 4, y: 8, z: 12 (z_hi: 2, z_lo: 6; z = z_hi * 6 + z_lo), core: 2. Of those that a mesh axis runs over, the one named last changes fastest.
Arguments:
- grad_out: bfloat16 [3072, 5120], P('ctx', 'tp'), may hold values from -6 to 6
- w_out: bfloat16 [4096, 5120], P('tp'), may hold values from -0.078125 to 0.078125
- query_proj: bfloat16 [3072, 4096], P('ctx', 'tp'), may hold values from -6 to 6
- key_proj: bfloat16 [3072, 4096], P('ctx', 'tp'), may hold values from -6 to 6
- value_proj: bfloat16 [3072, 4096], P('ctx', 'tp'), may hold values from -6 to 6
- w_query: bfloat16 [5120, 4096], P(None, 'tp'), may hold values from -0.1875 to 0.1875
- w_key: bfloat16 [5120, 4096], P(None, 'tp'), may hold values from -0.09375 to 0.09375
- w_value: bfloat16 [5120, 4096], P(None, 'tp'), may hold values from -0.09375 to 0.09375
- tile_keys: int32 [24, 13], replicated, may hold values from 0 to 23, as said below
Outputs:
- input_grad: float32 [5120, 3072], P('tp', 'ctx')
The draws below stay inside these ranges and needn't reach their ends.
Inputs may be any that keep to these rules, and one draw needn't show every extreme that they name: `tile_keys`: each row lists 13 distinct key tiles, among them the query tile itself; every listed tile u has |u - t| <= 12 for its query tile t.
All inputs are finite; a program needn't handle non-finite values.
Results may differ from the reference program's by a relative error of at most 0.0078.
Values may be sent and summed in bfloat16 or wider, within the bound.
A program may use at most 32 MiB of HBM per device.

```python
import jax
import jax.numpy as jnp
from jax import lax

D = 5120
HD = 128
TILE = 128
TILES_DEV = 1
HEADS = 32
TILES = 24
TOKENS = 3072
REACH = 12
KEEP = 13


def drawn_pair(key):
    base = jax.random.fold_in(key, 11)
    key_query, key_keys = jax.random.split(base, 2)
    shape = (TOKENS, HEADS * HD)
    queries = jnp.clip(jax.random.normal(key_query, shape, jnp.float32), -6.0, 6.0)
    keys_out = jnp.clip(jax.random.normal(key_keys, shape, jnp.float32), -6.0, 6.0)
    return (queries, keys_out)


def draw_query_proj(key, part):
    return drawn_pair(key)[0].astype(jnp.bfloat16)


def draw_key_proj(key, part):
    return drawn_pair(key)[1].astype(jnp.bfloat16)


def draw_tile_keys(key, part):
    tile_ids = jnp.arange(TILES, dtype=jnp.int32)
    time_rows = tile_ids // TILES_DEV
    inside = jnp.abs(time_rows[:, None] - time_rows[None, :]) <= REACH
    noise = jax.random.randint(jax.random.fold_in(key, 23), (TILES, TILES), 0, 2 ** 20)
    ranking = noise * TILES + tile_ids[None, :]
    ranking = jnp.where(inside, ranking, -1 - tile_ids[None, :])
    ranking = jnp.where(tile_ids[:, None] == tile_ids[None, :], 2 ** 30 + tile_ids[None, :], ranking)
    _, picked = lax.top_k(ranking, KEEP)
    return picked.astype(jnp.int32)


def spiked(values, stream_key, source, target, parts, factor):
    owner, partner = [(jnp.arange(values.shape[position]) // (values.shape[position] // parts)).reshape([-1 if axis == position else 1 for axis in range(values.ndim)]) for position in (source, target)]
    chosen = jax.random.permutation(stream_key, parts)[partner]
    strong = (owner == chosen) | (owner == (partner + parts // 2) % parts)
    return jnp.where(strong, factor * values, values)


def steps_of(stream_key, extent, cuts, low, largest):
    def one(axis_at, blocks):
        draws = jax.random.uniform(jax.random.fold_in(jax.random.fold_in(stream_key, 6), axis_at), (blocks,), jnp.float32, low / len(cuts), largest / len(cuts))
        return jnp.repeat(jnp.exp(draws), extent[axis_at] // blocks).reshape((-1,) + (1,) * (len(extent) - axis_at - 1))

    gain = one(*cuts[0])
    for cut in cuts[1:]:
        gain = gain * one(*cut)
    return gain


def gaussian(stream_key, shape, width, bound, cuts=(), held_as=jnp.bfloat16):
    loudness = steps_of(stream_key, shape, cuts, -0.22, 0.18) if cuts else 1.0
    drawn = jax.random.normal(stream_key, shape, jnp.float32) * width * loudness
    return jnp.minimum(jnp.maximum(drawn, -bound), bound).astype(held_as)


def heavy_noise(own_key, dims, width, most, cuts, heavy, kind=jnp.bfloat16):
    drawn = width * jax.random.normal(own_key, dims, jnp.float32)
    if cuts:
        drawn = drawn * steps_of(own_key, dims, cuts, -0.22, 0.18)
    return jnp.clip(spiked(drawn, jax.random.fold_in(own_key, 3), *heavy), -most, most).astype(kind)


def setup_inputs(seed: int = 0) -> dict:
    keys = jax.random.split(jax.random.key(seed), 10)
    return {
        "grad_out": gaussian(keys[0], (TOKENS, D), 1.0, 6.0, ((0, 24), (1, 32))),
        "w_out": gaussian(keys[1], (HEADS * HD, D), D ** -0.5, 0.078125, ((0, 32),)),
        "query_proj": draw_query_proj(jax.random.fold_in(keys[9], 71), 0),
        "key_proj": draw_key_proj(jax.random.fold_in(keys[9], 71), 0),
        "value_proj": gaussian(keys[4], (TOKENS, HEADS * HD), 1.0, 6.0, ((0, 24), (1, 32))),
        "w_query": heavy_noise(keys[5], (D, HEADS * HD), (HEADS * HD) ** -0.5, 0.1875, ((1, 32),), (1, 0, 32, 2.75)),
        "w_key": gaussian(keys[6], (D, HEADS * HD), (HEADS * HD) ** -0.5, 0.09375, ((1, 32),)),
        "w_value": gaussian(keys[7], (D, HEADS * HD), (HEADS * HD) ** -0.5, 0.09375, ((1, 32),)),
        "tile_keys": draw_tile_keys(jax.random.fold_in(keys[9], 71), 0),
    }


def head_gradient(head_index, grad_out, w_out, query_proj, key_proj, value_proj, w_query, w_key, w_value, token_mask):
    score_scale = HD ** -0.5
    head_start = head_index * HD
    out_rows = lax.dynamic_slice_in_dim(w_out, head_start, HD, 0)
    d_attn = lax.dot_general(grad_out, out_rows, (((1,), (1,)), ((), ())), preferred_element_type=jnp.float32).astype(jnp.bfloat16)
    queries = lax.dynamic_slice_in_dim(query_proj, head_start, HD, 1)
    keys_head = lax.dynamic_slice_in_dim(key_proj, head_start, HD, 1)
    values_head = lax.dynamic_slice_in_dim(value_proj, head_start, HD, 1)
    scores = lax.dot_general(queries, keys_head, (((1,), (1,)), ((), ())), preferred_element_type=jnp.float32) * score_scale
    scores = jnp.where(token_mask, scores, -jnp.inf)
    row_max = jnp.max(scores, axis=1, keepdims=True)
    exponent = jnp.exp(scores - row_max)
    row_total = jnp.sum(exponent, axis=1, keepdims=True)
    prob_exact = exponent / row_total
    prob_half = prob_exact.astype(jnp.bfloat16)
    attn_out = jnp.dot(prob_half, values_head, preferred_element_type=jnp.float32)
    row_delta = jnp.sum(d_attn.astype(jnp.float32) * attn_out, axis=1, keepdims=True)
    d_prob = lax.dot_general(d_attn, values_head, (((1,), (1,)), ((), ())), preferred_element_type=jnp.float32)
    d_score = (prob_exact * (d_prob - row_delta) * score_scale).astype(jnp.bfloat16)
    d_query = jnp.dot(d_score, keys_head, preferred_element_type=jnp.float32).astype(jnp.bfloat16)
    d_key = lax.dot_general(d_score, queries, (((0,), (0,)), ((), ())), preferred_element_type=jnp.float32).astype(jnp.bfloat16)
    d_value = lax.dot_general(prob_half, d_attn, (((0,), (0,)), ((), ())), preferred_element_type=jnp.float32).astype(jnp.bfloat16)
    query_cols = lax.dynamic_slice_in_dim(w_query, head_start, HD, 1)
    key_cols = lax.dynamic_slice_in_dim(w_key, head_start, HD, 1)
    value_cols = lax.dynamic_slice_in_dim(w_value, head_start, HD, 1)
    contract = (((1,), (1,)), ((), ()))
    head_term = lax.dot_general(query_cols, d_query, contract, preferred_element_type=jnp.float32)
    head_term = head_term + lax.dot_general(key_cols, d_key, contract, preferred_element_type=jnp.float32)
    head_term = head_term + lax.dot_general(value_cols, d_value, contract, preferred_element_type=jnp.float32)
    return head_term


def reference(grad_out, w_out, query_proj, key_proj, value_proj, w_query, w_key, w_value, tile_keys):
    tile_ids = jnp.arange(TILES, dtype=jnp.int32)
    tile_ok = jnp.any(tile_keys[:, :, None] == tile_ids[None, None, :], axis=1)
    token_mask = jnp.repeat(jnp.repeat(tile_ok, TILE, axis=0), TILE, axis=1)

    def scan_step(running, head_index):
        head_term = head_gradient(head_index, grad_out, w_out, query_proj, key_proj, value_proj, w_query, w_key, w_value, token_mask)
        return running + head_term, None

    running, _ = lax.scan(scan_step, jnp.zeros((D, TOKENS), jnp.float32), jnp.arange(HEADS, dtype=jnp.int32))
    return running
```

```python
import functools

import jax
import jax.numpy as jnp
from jax import lax
from jax.experimental import pallas as pl
from jax.experimental.pallas import tpu as pltpu
from jax.sharding import PartitionSpec as P

TILE = 128
X = 4
Z = 6
Y = 8
SPAN = 3
WAYS = 2 * SPAN + 1
MASKED = -1e30
MESH = pl.DeviceIdType.MESH
BF16 = jnp.bfloat16
F32 = jnp.float32
RELAY = {0: ((6, 1), (6, 2), (2, -1)), 1: ((2, -1), (2, -2), (6, 1))}
NEAR = (1, -1, 2, -2)
AG_SENDS = {e: tuple((0, step) for step in NEAR) + RELAY[e] for e in (0, 1)}
PLACE = {4: 0, 3: 1, 5: 2, 2: 3, 6: 4, 1: 5, 7: 6, 0: 7}


def dot(a, b):
    return jnp.dot(a, b, preferred_element_type=F32)


def dot_last(a, b):
    return lax.dot_general(a, b, (((1,), (1,)), ((), ())), preferred_element_type=F32)


def way(i):
    return ((i + 1) // 2) * (1 - 2 * ((i + 1) % 2))


def kernel(
    g_hbm, wo_hbm, q_hbm, k_hbm, v_hbm, wq_hbm, wk_hbm, wv_hbm, lists, out_ref,
    g_all, wo, qbuf, kall, vall, kt, vt, wcat,
    probs, stat_local, o_send, o_stat_send, o_recv, o_stat_recv,
    o_sum, m_sum, l_sum, do_buf, do_stat, dk_sum, dv_sum, dq_send, dq_recv, dq_sum,
    dkv_send, dkv_recv, d_cat, sib_out, sib_in, f_own, sum_out, relay_in, end_in, z_out, z_in,
    load_sem, ag_ss, ag_rs, ag_sib_ss, ag_sib_rs, pair_send, pair_recv,
    kv_ss, kv_rs, q_ss, q_rs, o_ss, o_rs, do_ss, do_rs, dq_ss, dq_rs, dkv_ss, dkv_rs,
    sib_ss, sib_rs, sum_ss, relay_rs, end_rs,
):
    ctx, tp = lax.axis_index("ctx"), lax.axis_index("tp")
    z, x = ctx // X, ctx % X
    half, y, core = tp // (2 * Y), (tp // 2) % Y, tp % 2
    scale = TILE ** (-0.5)
    block = out_ref.shape[0]
    listed = lists.shape[0]

    def tp_of(h, row, c):
        return h * (2 * Y) + row * 2 + c

    def half_of(e):
        return half if e == 0 else 1 - half

    def rows_of(h, row, c):
        return pl.ds(pl.multiple_of(tp_of(h, row, c) * block, block), block)

    def tile_rows(a):
        return pl.ds(pl.multiple_of(a * TILE, TILE), TILE)

    sibling = (ctx, tp_of(half, y, 1 - core))
    pair = (ctx, tp_of(1 - half, y, core))

    def y_peer(step):
        return (ctx, tp_of(half, (y + step + Y) % Y, core))

    def x_peer(j):
        return (z * X + (x + j) % X, tp)

    def z_peer(d):
        return ((z + d) * X + x, tp)

    def z_valid(d):
        return jnp.logical_and(z + d >= 0, z + d < Z)

    def remote(src, dst, ss, rs, to):
        return pltpu.make_async_remote_copy(
            src_ref=src, dst_ref=dst, send_sem=ss, recv_sem=rs, device_id=to, device_id_type=MESH
        )

    loads = [
        pltpu.make_async_copy(src, dst, load_sem.at[n])
        for n, (src, dst) in enumerate((
            (g_hbm, g_all.at[rows_of(half, y, core)]),
            (k_hbm, kall.at[tile_rows(x)]),
            (v_hbm, vall.at[tile_rows(x)]),
            (q_hbm, qbuf.at[SPAN]),
            (wo_hbm, wo),
            (wq_hbm, wcat.at[:, 0:TILE]),
            (wk_hbm, wcat.at[:, TILE : 2 * TILE]),
            (wv_hbm, wcat.at[:, 2 * TILE : 3 * TILE]),
        ))
    ]
    for load in loads:
        load.start()

    barrier = pltpu.get_barrier_semaphore()
    for to in (sibling, pair, *map(y_peer, NEAR), x_peer(1), x_peer(2), x_peer(3)):
        pl.semaphore_signal(barrier, inc=1, device_id=to, device_id_type=MESH)
    expected = jnp.int32(9)
    for d in (1, -1, 2, -2, 3, -3):
        @pl.when(z_valid(d))
        def _():
            pl.semaphore_signal(barrier, inc=1, device_id=z_peer(d), device_id_type=MESH)

        expected = expected + jnp.where(z_valid(d), 1, 0)

    loads[0].wait()
    pl.semaphore_wait(barrier, expected)

    def ag_slot(e, rel):
        return g_all.at[rows_of(half_of(e), (y + rel) % Y, core)]

    def ag_send(e, n):
        rel, step = AG_SENDS[e][n]
        slot = ag_slot(e, rel)
        return remote(slot, slot, ag_ss.at[e, n], ag_rs.at[e, (rel - step) % Y], y_peer(step))

    def ag_sib(e, rel):
        slot = ag_slot(e, rel)
        return remote(slot, slot, ag_sib_ss.at[e, rel], ag_sib_rs.at[e, rel], sibling)

    def ag_sib_wait(e):
        for rel in (0, 1, 7, 2, 6, 3, 5, 4):
            slot = g_all.at[rows_of(half_of(e), (y + rel) % Y, 1 - core)]
            remote(slot, slot, ag_sib_ss.at[e, rel], ag_sib_rs.at[e, rel], sibling).wait_recv()

    def ag_own(e):
        for n in range(len(NEAR)):
            ag_send(e, n).start()
        ag_sib(e, 0).start()

    def ag_arrive(e, rels):
        for rel in rels:
            slot = ag_slot(e, rel)
            remote(slot, slot, ag_ss.at[e, 0], ag_rs.at[e, rel], y_peer(1)).wait_recv()
            for n, (source, _) in enumerate(AG_SENDS[e]):
                if source == rel:
                    ag_send(e, n).start()
            ag_sib(e, rel).start()

    own_slot = ag_slot(0, 0)
    other_slot = ag_slot(1, 0)
    pair_copy = remote(own_slot, own_slot, pair_send.at[0], pair_recv.at[0], pair)
    pair_copy.start()
    ag_own(0)
    for load in loads[1:4]:
        load.wait()

    def kv_copy(buf, which, j):
        slot = buf.at[tile_rows(x)]
        return remote(slot, slot, kv_ss.at[which, j], kv_rs.at[which, x], x_peer(j))

    for j in (1, 3, 2):
        kv_copy(kall, 0, j).start()
        kv_copy(vall, 1, j).start()

    def q_copy(d):
        return remote(qbuf.at[SPAN], qbuf.at[SPAN - d], q_ss.at[SPAN + d], q_rs.at[SPAN - d], z_peer(d))

    for d in (1, -1, 2, -2, 3, -3):
        @pl.when(z_valid(d))
        def _():
            q_copy(d).start()

    ag_arrive(0, (2, 6, 1, 7))

    for j in (1, 3, 2):
        source = (x + j) % X
        for which, buf in ((0, kall), (1, vall)):
            slot = buf.at[tile_rows(source)]
            remote(slot, slot, kv_ss.at[which, j], kv_rs.at[which, source], x_peer(j)).wait_recv()
    for a in range(X):
        part = slice(a * TILE, (a + 1) * TILE)
        kt[:, part] = kall[part, :].astype(F32).T.astype(BF16)
        vt[:, part] = vall[part, :].astype(F32).T.astype(BF16)

    row_index = lax.broadcasted_iota(jnp.int32, (8, TILE), 0)

    def o_copy(which, d):
        send, recv = ((o_send, o_recv), (o_stat_send, o_stat_recv))[which]
        return remote(
            send.at[SPAN + d], recv.at[SPAN - d], o_ss.at[which, SPAN + d], o_rs.at[which, SPAN - d], z_peer(d)
        )

    def scores_of(i, carry):
        d = way(i)

        @pl.when(z_valid(d))
        def _():
            @pl.when(d != 0)
            def _():
                q_copy(-d).wait_recv()

            tile = (z + d) * X + x
            s = dot_last(kall[...], qbuf[SPAN + d])
            parts = []
            for a in range(X):
                key_tile = z * X + a
                found = lists[0, tile] == key_tile
                for n in range(1, listed):
                    found = jnp.logical_or(found, lists[n, tile] == key_tile)
                bias = jnp.where(found, jnp.float32(0.0), jnp.float32(MASKED))
                parts.append(s[a * TILE : (a + 1) * TILE] * scale + bias)
            top = functools.reduce(jnp.maximum, parts)
            row_max = jnp.max(top, axis=0, keepdims=True)
            parts = [jnp.exp(part - row_max) for part in parts]
            row_total = jnp.sum(functools.reduce(jnp.add, parts), axis=0, keepdims=True)
            for a in range(X):
                probs[SPAN + d, a * TILE : (a + 1) * TILE, :] = parts[a]
            stat = jnp.where(row_index == 0, row_max, row_total)
            stat_local[SPAN + d] = stat
            o_part = dot(vt[...], jnp.concatenate([part.astype(BF16) for part in parts], axis=0))

            @pl.when(d == 0)
            def _():
                o_sum[...] = o_part
                m_sum[...] = row_max
                l_sum[...] = row_total

            @pl.when(d != 0)
            def _():
                o_send[SPAN + d] = o_part.astype(BF16)
                o_stat_send[SPAN + d] = stat
                o_copy(0, d).start()
                o_copy(1, d).start()

        return carry

    remote(other_slot, other_slot, pair_send.at[0], pair_recv.at[0], pair).wait_recv()
    ag_own(1)
    lax.fori_loop(0, 1, scores_of, 0)
    ag_arrive(0, (3, 5, 4))
    lax.fori_loop(1, 3, scores_of, 0)
    ag_arrive(1, (2, 6, 1, 7))
    lax.fori_loop(3, 7, scores_of, 0)
    ag_arrive(1, (3, 5, 4))

    def merge(i, carry):
        d = way(i)

        @pl.when(z_valid(d))
        def _():
            o_copy(0, -d).wait_recv()
            o_copy(1, -d).wait_recv()
            m_part = o_stat_recv[SPAN + d, 0:1, :]
            l_part = o_stat_recv[SPAN + d, 1:2, :]
            m_old = m_sum[...]
            m_new = jnp.maximum(m_old, m_part)
            w_old, w_part = jnp.exp(m_old - m_new), jnp.exp(m_part - m_new)
            m_sum[...] = m_new
            l_sum[...] = l_sum[...] * w_old + l_part * w_part
            o_sum[...] = o_sum[...] * w_old + o_recv[SPAN + d].astype(F32) * w_part

        return carry

    def d_attn_of(e):
        ag_sib_wait(e)
        span = Y * 2 * block
        part = pl.ds(pl.multiple_of(half_of(e) * span, TILE), span)
        return dot(wo[:, part], g_all[part, :])

    loads[4].wait()
    d_out = d_attn_of(0)
    lax.fori_loop(1, WAYS, merge, 0)
    d_out = (d_out + d_attn_of(1)).astype(BF16)
    do_buf[SPAN] = d_out
    inverse = 1.0 / l_sum[...]
    delta = jnp.sum(d_out.astype(F32) * o_sum[...], axis=0, keepdims=True) * inverse
    do_stat[SPAN] = jnp.where(row_index == 0, m_sum[...], jnp.where(row_index == 1, inverse, delta))

    def do_copy(which, d):
        buf = (do_buf, do_stat)[which]
        return remote(
            buf.at[SPAN], buf.at[SPAN - d], do_ss.at[which, SPAN + d], do_rs.at[which, SPAN - d], z_peer(d)
        )

    for d in (1, -1, 2, -2, 3, -3):
        @pl.when(z_valid(d))
        def _():
            do_copy(0, d).start()
            do_copy(1, d).start()

    def dq_copy(d):
        return remote(dq_send.at[SPAN + d], dq_recv.at[SPAN - d], dq_ss.at[SPAN + d], dq_rs.at[SPAN - d], z_peer(d))

    dk_sum[...] = jnp.zeros_like(dk_sum)
    dv_sum[...] = jnp.zeros_like(dv_sum)

    def gradients_of(i, carry):
        d = way(i)

        @pl.when(z_valid(d))
        def _():
            @pl.when(d != 0)
            def _():
                do_copy(0, -d).wait_recv()
                do_copy(1, -d).wait_recv()

            row_max = do_stat[SPAN + d, 0:1, :]
            inv = do_stat[SPAN + d, 1:2, :]
            row_delta = do_stat[SPAN + d, 2:3, :]
            weight = jnp.exp(stat_local[SPAN + d, 0:1, :] - row_max) * inv
            d_o = do_buf[SPAN + d]
            prob = probs[SPAN + d] * weight
            d_prob = dot(vall[...], d_o)
            d_score = (prob * (d_prob - row_delta) * scale).astype(BF16)
            dv_sum[...] += dot_last(prob.astype(BF16), d_o)
            dk_sum[...] += dot(d_score, qbuf[SPAN + d])
            d_q = dot(kt[...], d_score)

            @pl.when(d == 0)
            def _():
                dq_sum[...] = d_q

            @pl.when(d != 0)
            def _():
                dq_send[SPAN + d] = d_q.astype(BF16)
                dq_copy(d).start()

        return carry

    lax.fori_loop(0, WAYS, gradients_of, 0)

    def dkv_copy(j):
        return remote(dkv_send.at[j], dkv_recv.at[j], dkv_ss.at[j], dkv_rs.at[j], x_peer(j))

    for j in (1, 3, 2):
        tile = tile_rows((x + j) % X)
        dkv_send[j, 0:TILE, :] = dk_sum[tile, :].astype(BF16)
        dkv_send[j, TILE : 2 * TILE, :] = dv_sum[tile, :].astype(BF16)
        dkv_copy(j).start()

    def dq_add(i, carry):
        d = way(i)

        @pl.when(z_valid(d))
        def _():
            dq_copy(-d).wait_recv()
            dq_sum[...] += dq_recv[SPAN + d].astype(F32)

        return carry

    d_key = dk_sum[tile_rows(x), :]
    d_value = dv_sum[tile_rows(x), :]
    lax.fori_loop(1, WAYS, dq_add, 0)
    for j in (1, 3, 2):
        dkv_copy(j).wait_recv()
        d_key = d_key + dkv_recv[j, 0:TILE, :].astype(F32)
        d_value = d_value + dkv_recv[j, TILE : 2 * TILE, :].astype(F32)
    d_cat[0:TILE, :] = dq_sum[...].astype(BF16)
    d_cat[TILE : 2 * TILE, :] = d_key.T.astype(BF16)
    d_cat[2 * TILE : 3 * TILE, :] = d_value.T.astype(BF16)
    for load in loads[5:]:
        load.wait()

    def features(j, carry):
        rel = (4 + ((j + 1) // 2) * (1 - 2 * (j % 2))) % Y
        for e in (1, 0):
            start = pl.multiple_of(tp_of(half_of(e), (y + rel) % Y, 0) * block, block)
            both = dot(wcat[pl.ds(start, 2 * block), :], d_cat[...])
            first, second = both[:block], both[block:]
            f_own[j, e] = jnp.where(core == 0, first, second)
            sib_out[j, e] = jnp.where(core == 0, second, first).astype(BF16)
        sib_copy(j).start()
        return carry

    def sib_copy(j):
        return remote(sib_out.at[j], sib_in.at[j], sib_ss.at[j], sib_rs.at[j], sibling)

    def summed(e, rel):
        return f_own[PLACE[rel], e] + sib_in[PLACE[rel], e].astype(F32)

    def relay_wait(e, way_in):
        remote(
            sum_out.at[e, way_in], relay_in.at[e, way_in], sum_ss.at[e, way_in], relay_rs.at[e, way_in], y_peer(1)
        ).wait_recv()
        return relay_in[e, way_in].astype(F32)

    def sum_copy(e, n):
        step = ((-1, 1, (-2, 2)[e]) + (-2, 2, -1, 1))[n]
        dst, sem = (relay_in.at[e, n], relay_rs.at[e, n]) if n < 3 else (end_in.at[e, n - 3], end_rs.at[e, n - 3])
        return remote(sum_out.at[e, n], dst, sum_ss.at[e, n], sem, y_peer(step))

    def sum_send(e, n, value):
        sum_out[e, n] = value.astype(BF16)
        sum_copy(e, n).start()

    lax.fori_loop(0, 4, features, 0)
    for j in (0, 1, 2):
        sib_copy(j).wait_recv()
    for e in (1, 0):
        sum_send(e, 2, summed(e, 4))
        sum_send(e, 0, summed(e, 5))
        sum_send(e, 1, summed(e, 3))
    lax.fori_loop(4, 8, features, 0)
    for j in (3, 4, 5, 6, 7):
        sib_copy(j).wait_recv()
    for e in (1, 0):
        sum_send(e, 5, summed(e, 7))
        sum_send(e, 6, summed(e, 1))
    for e in (1, 0):
        for n, rel in ((3, 6), (4, 2)):
            value = summed(e, rel) + relay_wait(e, n - 3)
            if n - 3 == e:
                value = value + relay_wait(e, 2)
            sum_send(e, n, value)

    def sum_end(e):
        value = summed(e, 0)
        for n in (2, 3, 0, 1):
            remote(
                sum_out.at[e, n + 3], end_in.at[e, n], sum_ss.at[e, n + 3], end_rs.at[e, n], y_peer(1)
            ).wait_recv()
            value = value + end_in[e, n].astype(F32)
        return value

    z_out[...] = sum_end(1).astype(BF16)
    pair_sum = remote(z_out, z_in, pair_send.at[1], pair_recv.at[1], pair)
    pair_sum.start()
    out_ref[...] = sum_end(0)

    pair_copy.wait_send()
    for e in (0, 1):
        for n in range(7):
            ag_send(e, n).wait_send()
            sum_copy(e, n).wait_send()
        for rel in range(Y):
            ag_sib(e, rel).wait_send()
    for j in (1, 2, 3):
        kv_copy(kall, 0, j).wait_send()
        kv_copy(vall, 1, j).wait_send()
        dkv_copy(j).wait_send()

    def drain(i, carry):
        d = way(i)

        @pl.when(z_valid(d))
        def _():
            q_copy(d).wait_send()
            dq_copy(d).wait_send()
            for which in (0, 1):
                o_copy(which, d).wait_send()
                do_copy(which, d).wait_send()

        return carry

    lax.fori_loop(1, WAYS, drain, 0)

    def drain_sibling(i, carry):
        sib_copy(i).wait_send()
        return carry

    lax.fori_loop(0, Y, drain_sibling, 0)
    pair_sum.wait()
    out_ref[...] += z_in[...].astype(F32)


def on_device(
    grad_out, w_out, query_proj, key_proj, value_proj, w_query, w_key, w_value, tile_keys
):
    block = grad_out.shape[1]
    features = w_out.shape[1]
    dma = pltpu.SemaphoreType.DMA
    square = (TILE, TILE)
    column = (X * TILE, TILE)
    row = (1, TILE)
    stat = (WAYS, 8, TILE)
    piece = (block, TILE)
    anywhere = pl.BlockSpec(memory_space=pl.ANY)
    return pl.pallas_call(
        kernel,
        out_shape=jax.ShapeDtypeStruct(piece, F32),
        in_specs=[anywhere] * 8 + [pl.BlockSpec(memory_space=pltpu.SMEM)],
        out_specs=pl.BlockSpec(memory_space=pltpu.VMEM),
        scratch_shapes=[
            pltpu.VMEM((features, TILE), BF16),
            pltpu.VMEM(w_out.shape, BF16),
            pltpu.VMEM((WAYS, *square), BF16),
            pltpu.VMEM(column, BF16),
            pltpu.VMEM(column, BF16),
            pltpu.VMEM(column[::-1], BF16),
            pltpu.VMEM(column[::-1], BF16),
            pltpu.VMEM((features, 3 * TILE), BF16),
            pltpu.VMEM((WAYS, *column), F32),
            pltpu.VMEM(stat, F32),
            pltpu.VMEM((WAYS, *square), BF16),
            pltpu.VMEM(stat, F32),
            pltpu.VMEM((WAYS, *square), BF16),
            pltpu.VMEM(stat, F32),
            pltpu.VMEM(square, F32),
            pltpu.VMEM(row, F32),
            pltpu.VMEM(row, F32),
            pltpu.VMEM((WAYS, *square), BF16),
            pltpu.VMEM(stat, F32),
            pltpu.VMEM(column, F32),
            pltpu.VMEM(column, F32),
            pltpu.VMEM((WAYS, *square), BF16),
            pltpu.VMEM((WAYS, *square), BF16),
            pltpu.VMEM(square, F32),
            pltpu.VMEM((X, 2 * TILE, TILE), BF16),
            pltpu.VMEM((X, 2 * TILE, TILE), BF16),
            pltpu.VMEM((3 * TILE, TILE), BF16),
            pltpu.VMEM((Y, 2, *piece), BF16),
            pltpu.VMEM((Y, 2, *piece), BF16),
            pltpu.VMEM((Y, 2, *piece), F32),
            pltpu.VMEM((2, 7, *piece), BF16),
            pltpu.VMEM((2, 3, *piece), BF16),
            pltpu.VMEM((2, 4, *piece), BF16),
            pltpu.VMEM(piece, BF16),
            pltpu.VMEM(piece, BF16),
            dma((8,)),
            dma((2, 7)), dma((2, Y)),
            dma((2, Y)), dma((2, Y)),
            dma((2,)), dma((2,)),
            dma((2, X)), dma((2, X)),
            dma((WAYS,)), dma((WAYS,)),
            dma((2, WAYS)), dma((2, WAYS)),
            dma((2, WAYS)), dma((2, WAYS)),
            dma((WAYS,)), dma((WAYS,)),
            dma((X,)), dma((X,)),
            dma((Y,)), dma((Y,)),
            dma((2, 7)), dma((2, 3)), dma((2, 4)),
        ],
        compiler_params=pltpu.CompilerParams(
            collective_id=0, has_side_effects=True, vmem_limit_bytes=60 * 1024 * 1024
        ),
    )(grad_out.T, w_out, query_proj, key_proj, value_proj, w_query, w_key, w_value, tile_keys.T)


def solution(mesh):
    return jax.shard_map(
        on_device,
        mesh=mesh,
        in_specs=(
            P("ctx", "tp"),
            P("tp", None),
            P("ctx", "tp"),
            P("ctx", "tp"),
            P("ctx", "tp"),
            P(None, "tp"),
            P(None, "tp"),
            P(None, "tp"),
            P(),
        ),
        out_specs=P("tp", "ctx"),
        check_vma=False,
    )
```

```python
import functools

import jax
import jax.numpy as jnp
from jax import lax
from jax.experimental import pallas as pl
from jax.experimental.pallas import tpu as pltpu
from jax.sharding import PartitionSpec as P

TILE = 128
X = 4
Z = 6
Y = 8
SPAN = 3
WAYS = 2 * SPAN + 1
MASKED = -1e30
MESH = pl.DeviceIdType.MESH
BF16 = jnp.bfloat16
F32 = jnp.float32
NEAR = (1, -1, 2, -2)
AG_SENDS = {
    0: tuple((0, step) for step in NEAR) + ((6, 1), (6, 2), (2, -1)),
    1: tuple((0, step) for step in NEAR) + ((4, 1), (4, -1)),
}
SUM_STEPS = {0: (-1, 1, -2, -2, 2, -1, 1), 1: (1, -1, None, -2, 2, -1, 1)}
SUM_SENDS = {e: tuple(n for n in range(7) if SUM_STEPS[e][n] is not None) for e in (0, 1)}
PLACE = {4: 0, 3: 1, 5: 2, 2: 3, 6: 4, 1: 5, 7: 6, 0: 7}


def dot(a, b):
    return jnp.dot(a, b, preferred_element_type=F32)


def dot_last(a, b):
    return lax.dot_general(a, b, (((1,), (1,)), ((), ())), preferred_element_type=F32)


def way(i):
    return ((i + 1) // 2) * (1 - 2 * ((i + 1) % 2))


def far_way(i):
    return ((i + WAYS - 1) // WAYS) * (SPAN + 1 - (i + 1) // 2) * (1 - 2 * ((i + 1) % 2))


def kernel(
    g_hbm, wo_hbm, q_hbm, k_hbm, v_hbm, wq_hbm, wk_hbm, wv_hbm, lists, out_ref,
    g_all, wo, qbuf, kall, vall, kt, vt, wcat,
    probs, stat_local, o_send, o_stat_send, o_recv, o_stat_recv,
    o_sum, m_sum, l_sum, do_buf, do_stat, dk_sum, dv_sum, dq_send, dq_recv, dq_sum,
    dkv_send, dkv_recv, d_cat, sib_out, sib_in, f_own, sum_out, relay_in, end_in, z_out, z_in,
    load_sem, ag_ss, ag_rs, ag_sib_ss, ag_sib_rs, pair_ss, pair_rs,
    kv_ss, kv_rs, q_ss, q_rs, o_ss, o_rs, do_ss, do_rs, dq_ss, dq_rs, dkv_ss, dkv_rs,
    sib_ss, sib_rs, sum_ss, relay_rs, end_rs,
):
    ctx, tp = lax.axis_index("ctx"), lax.axis_index("tp")
    z, x = ctx // X, ctx % X
    half, y, core = tp // (2 * Y), (tp // 2) % Y, tp % 2
    scale = TILE ** (-0.5)
    block = out_ref.shape[0]
    listed = lists.shape[0]

    def tp_of(h, row, c):
        return h * (2 * Y) + row * 2 + c

    def half_of(e):
        return half if e == 0 else 1 - half

    def rows_of(h, row, c):
        return pl.ds(pl.multiple_of(tp_of(h, row, c) * block, block), block)

    def tile_rows(a):
        return pl.ds(pl.multiple_of(a * TILE, TILE), TILE)

    sibling = (ctx, tp_of(half, y, 1 - core))
    pairs = ((ctx, tp_of(1 - half, y, core)), (ctx, tp_of(1 - half, (y + Y // 2) % Y, core)))

    def y_peer(step):
        return (ctx, tp_of(half, (y + step + Y) % Y, core))

    def x_peer(j):
        return (z * X + (x + j) % X, tp)

    def z_peer(d):
        return ((z + d) * X + x, tp)

    def z_valid(d):
        return jnp.logical_and(z + d >= 0, z + d < Z)

    def remote(src, dst, ss, rs, to):
        return pltpu.make_async_remote_copy(
            src_ref=src, dst_ref=dst, send_sem=ss, recv_sem=rs, device_id=to, device_id_type=MESH
        )

    loads = [
        pltpu.make_async_copy(src, dst, load_sem.at[n])
        for n, (src, dst) in enumerate((
            (g_hbm, g_all.at[rows_of(half, y, core)]),
            (k_hbm, kall.at[tile_rows(x)]),
            (v_hbm, vall.at[tile_rows(x)]),
            (q_hbm, qbuf.at[SPAN]),
            (wo_hbm, wo),
            (wq_hbm, wcat.at[:, 0:TILE]),
            (wk_hbm, wcat.at[:, TILE : 2 * TILE]),
            (wv_hbm, wcat.at[:, 2 * TILE : 3 * TILE]),
        ))
    ]
    for load in loads:
        load.start()

    barrier = pltpu.get_barrier_semaphore()
    for to in (sibling, *pairs, *map(y_peer, NEAR), x_peer(1), x_peer(2), x_peer(3)):
        pl.semaphore_signal(barrier, inc=1, device_id=to, device_id_type=MESH)
    expected = jnp.int32(10)
    for d in (1, -1, 2, -2, 3, -3):
        @pl.when(z_valid(d))
        def _():
            pl.semaphore_signal(barrier, inc=1, device_id=z_peer(d), device_id_type=MESH)

        expected = expected + jnp.where(z_valid(d), 1, 0)

    loads[0].wait()
    pl.semaphore_wait(barrier, expected)

    def ag_slot(e, rel):
        return g_all.at[rows_of(half_of(e), (y + rel) % Y, core)]

    def ag_send(e, n):
        rel, step = AG_SENDS[e][n]
        slot = ag_slot(e, rel)
        return remote(slot, slot, ag_ss.at[e, n], ag_rs.at[e, (rel - step) % Y], y_peer(step))

    def ag_sib(e, rel):
        slot = ag_slot(e, rel)
        return remote(slot, slot, ag_sib_ss.at[e, rel], ag_sib_rs.at[e, rel], sibling)

    def ag_sib_wait(e):
        for rel in (0, 1, 7, 2, 6, 3, 5, 4):
            slot = g_all.at[rows_of(half_of(e), (y + rel) % Y, 1 - core)]
            remote(slot, slot, ag_sib_ss.at[e, rel], ag_sib_rs.at[e, rel], sibling).wait_recv()

    def ag_own(e):
        for n in range(len(NEAR)):
            ag_send(e, n).start()
        ag_sib(e, 0).start()

    def ag_arrive(e, rels):
        for rel in rels:
            slot = ag_slot(e, rel)
            remote(slot, slot, ag_ss.at[e, 0], ag_rs.at[e, rel], y_peer(1)).wait_recv()
            for n, (source, _) in enumerate(AG_SENDS[e]):
                if source == rel:
                    ag_send(e, n).start()
            ag_sib(e, rel).start()

    def pair_copy(n):
        slot = ag_slot(0, 0)
        return remote(slot, slot, pair_ss.at[n], pair_rs.at[n], pairs[n])

    def pair_wait(n):
        slot = ag_slot(1, n * (Y // 2))
        remote(slot, slot, pair_ss.at[n], pair_rs.at[n], pairs[n]).wait_recv()

    pair_copy(0).start()
    pair_copy(1).start()
    for load in loads[1:4]:
        load.wait()

    def q_copy(d):
        return remote(qbuf.at[SPAN], qbuf.at[SPAN - d], q_ss.at[SPAN + d], q_rs.at[SPAN - d], z_peer(d))

    for d in (3, -3, 2, -2, 1, -1):
        @pl.when(z_valid(d))
        def _():
            q_copy(d).start()

    def kv_copy(buf, which, j):
        slot = buf.at[tile_rows(x)]
        return remote(slot, slot, kv_ss.at[which, j], kv_rs.at[which, x], x_peer(j))

    for j in (1, 3, 2):
        kv_copy(kall, 0, j).start()
        kv_copy(vall, 1, j).start()

    ag_own(0)

    ag_arrive(0, (2, 6, 1, 7))

    for j in (1, 3, 2):
        source = (x + j) % X
        for which, buf in ((0, kall), (1, vall)):
            slot = buf.at[tile_rows(source)]
            remote(slot, slot, kv_ss.at[which, j], kv_rs.at[which, source], x_peer(j)).wait_recv()
    for a in range(X):
        part = slice(a * TILE, (a + 1) * TILE)
        kt[:, part] = kall[part, :].astype(F32).T.astype(BF16)
        vt[:, part] = vall[part, :].astype(F32).T.astype(BF16)

    row_index = lax.broadcasted_iota(jnp.int32, (8, TILE), 0)

    def o_copy(which, d):
        send, recv = ((o_send, o_recv), (o_stat_send, o_stat_recv))[which]
        return remote(
            send.at[SPAN + d], recv.at[SPAN - d], o_ss.at[which, SPAN + d], o_rs.at[which, SPAN - d], z_peer(d)
        )

    def scores_of(i, carry):
        d = far_way(i)

        @pl.when(z_valid(d))
        def _():
            @pl.when(d != 0)
            def _():
                q_copy(-d).wait_recv()

            tile = (z + d) * X + x
            s = dot_last(kall[...], qbuf[SPAN + d])
            parts = []
            for a in range(X):
                key_tile = z * X + a
                found = lists[0, tile] == key_tile
                for n in range(1, listed):
                    found = jnp.logical_or(found, lists[n, tile] == key_tile)
                bias = jnp.where(found, jnp.float32(0.0), jnp.float32(MASKED))
                parts.append(s[a * TILE : (a + 1) * TILE] * scale + bias)
            top = functools.reduce(jnp.maximum, parts)
            row_max = jnp.max(top, axis=0, keepdims=True)
            parts = [jnp.exp(part - row_max) for part in parts]
            row_total = jnp.sum(functools.reduce(jnp.add, parts), axis=0, keepdims=True)
            for a in range(X):
                probs[SPAN + d, a * TILE : (a + 1) * TILE, :] = parts[a]
            stat = jnp.where(row_index == 0, row_max, row_total)
            stat_local[SPAN + d] = stat
            o_part = dot(vt[...], jnp.concatenate([part.astype(BF16) for part in parts], axis=0))

            @pl.when(d == 0)
            def _():
                o_sum[...] = o_part
                m_sum[...] = row_max
                l_sum[...] = row_total

            @pl.when(d != 0)
            def _():
                o_send[SPAN + d] = o_part.astype(BF16)
                o_stat_send[SPAN + d] = stat
                o_copy(0, d).start()
                o_copy(1, d).start()

        return carry

    lax.fori_loop(0, 1, scores_of, 0)
    pair_wait(0)
    ag_own(1)
    lax.fori_loop(1, 5, scores_of, 0)
    pair_wait(1)
    for n in (4, 5):
        ag_send(1, n).start()
    ag_sib(1, 4).start()
    lax.fori_loop(5, 7, scores_of, 0)
    ag_arrive(0, (3, 5, 4))
    ag_arrive(1, (2, 6, 1, 7))
    ag_arrive(1, (3, 5))

    def merge(i, carry):
        d = way(i)

        @pl.when(z_valid(d))
        def _():
            o_copy(0, -d).wait_recv()
            o_copy(1, -d).wait_recv()
            m_part = o_stat_recv[SPAN + d, 0:1, :]
            l_part = o_stat_recv[SPAN + d, 1:2, :]
            m_old = m_sum[...]
            m_new = jnp.maximum(m_old, m_part)
            w_old, w_part = jnp.exp(m_old - m_new), jnp.exp(m_part - m_new)
            m_sum[...] = m_new
            l_sum[...] = l_sum[...] * w_old + l_part * w_part
            o_sum[...] = o_sum[...] * w_old + o_recv[SPAN + d].astype(F32) * w_part

        return carry

    def d_attn_of(e):
        ag_sib_wait(e)
        span = Y * 2 * block
        part = pl.ds(pl.multiple_of(half_of(e) * span, TILE), span)
        return dot(wo[:, part], g_all[part, :])

    loads[4].wait()
    d_out = d_attn_of(0)
    lax.fori_loop(1, WAYS, merge, 0)
    d_out = (d_out + d_attn_of(1)).astype(BF16)
    do_buf[SPAN] = d_out
    inverse = 1.0 / l_sum[...]
    delta = jnp.sum(d_out.astype(F32) * o_sum[...], axis=0, keepdims=True) * inverse
    do_stat[SPAN] = jnp.where(row_index == 0, m_sum[...], jnp.where(row_index == 1, inverse, delta))

    def do_copy(which, d):
        buf = (do_buf, do_stat)[which]
        return remote(
            buf.at[SPAN], buf.at[SPAN - d], do_ss.at[which, SPAN + d], do_rs.at[which, SPAN - d], z_peer(d)
        )

    for d in (3, -3, 2, -2, 1, -1):
        @pl.when(z_valid(d))
        def _():
            do_copy(0, d).start()
            do_copy(1, d).start()

    def dq_copy(d):
        return remote(dq_send.at[SPAN + d], dq_recv.at[SPAN - d], dq_ss.at[SPAN + d], dq_rs.at[SPAN - d], z_peer(d))

    dk_sum[...] = jnp.zeros_like(dk_sum)
    dv_sum[...] = jnp.zeros_like(dv_sum)

    def gradients_of(i, carry):
        d = far_way(i)

        @pl.when(z_valid(d))
        def _():
            @pl.when(d != 0)
            def _():
                do_copy(0, -d).wait_recv()
                do_copy(1, -d).wait_recv()

            row_max = do_stat[SPAN + d, 0:1, :]
            inv = do_stat[SPAN + d, 1:2, :]
            row_delta = do_stat[SPAN + d, 2:3, :]
            weight = jnp.exp(stat_local[SPAN + d, 0:1, :] - row_max) * inv
            d_o = do_buf[SPAN + d]
            prob = probs[SPAN + d] * weight
            d_prob = dot(vall[...], d_o)
            d_score = (prob * (d_prob - row_delta) * scale).astype(BF16)
            dv_sum[...] += dot_last(prob.astype(BF16), d_o)
            dk_sum[...] += dot(d_score, qbuf[SPAN + d])
            d_q = dot(kt[...], d_score)

            @pl.when(d == 0)
            def _():
                dq_sum[...] = d_q

            @pl.when(d != 0)
            def _():
                dq_send[SPAN + d] = d_q.astype(BF16)
                dq_copy(d).start()

        return carry

    lax.fori_loop(0, WAYS, gradients_of, 0)

    def dkv_copy(j):
        return remote(dkv_send.at[j], dkv_recv.at[j], dkv_ss.at[j], dkv_rs.at[j], x_peer(j))

    for j in (1, 3, 2):
        tile = tile_rows((x + j) % X)
        dkv_send[j, 0:TILE, :] = dk_sum[tile, :].astype(BF16)
        dkv_send[j, TILE : 2 * TILE, :] = dv_sum[tile, :].astype(BF16)
        dkv_copy(j).start()

    def dq_add(i, carry):
        d = way(i)

        @pl.when(z_valid(d))
        def _():
            dq_copy(-d).wait_recv()
            dq_sum[...] += dq_recv[SPAN + d].astype(F32)

        return carry

    d_key = dk_sum[tile_rows(x), :]
    d_value = dv_sum[tile_rows(x), :]
    lax.fori_loop(1, WAYS, dq_add, 0)
    for j in (1, 3, 2):
        dkv_copy(j).wait_recv()
        d_key = d_key + dkv_recv[j, 0:TILE, :].astype(F32)
        d_value = d_value + dkv_recv[j, TILE : 2 * TILE, :].astype(F32)
    d_cat[0:TILE, :] = dq_sum[...].astype(BF16)
    d_cat[TILE : 2 * TILE, :] = d_key.T.astype(BF16)
    d_cat[2 * TILE : 3 * TILE, :] = d_value.T.astype(BF16)
    for load in loads[5:]:
        load.wait()

    def features(e, m, carry):
        for n, rel in enumerate((4 + m, 3 - m)):
            start = pl.multiple_of(tp_of(half_of(e), (y + rel) % Y, 0) * block, block)
            both = dot(wcat[pl.ds(start, 2 * block), :], d_cat[...])
            first, second = both[:block], both[block:]
            f_own[e, m, n] = jnp.where(core == 0, first, second)
            sib_out[e, m, n] = jnp.where(core == 0, second, first).astype(BF16)
        sib_copy(e, m).start()
        return carry

    def sib_copy(e, m):
        return remote(sib_out.at[e, m], sib_in.at[e, m], sib_ss.at[e, m], sib_rs.at[e, m], sibling)

    def summed(e, rel):
        m, n = PLACE[rel] // 2, PLACE[rel] % 2
        return f_own[e, m, n] + sib_in[e, m, n].astype(F32)

    def relay_wait(e, way_in):
        remote(
            sum_out.at[e, way_in], relay_in.at[e, way_in], sum_ss.at[e, way_in], relay_rs.at[e, way_in], y_peer(1)
        ).wait_recv()
        return relay_in[e, way_in].astype(F32)

    def sum_copy(e, n):
        dst, sem = (relay_in.at[e, n], relay_rs.at[e, n]) if n < 3 else (end_in.at[e, n - 3], end_rs.at[e, n - 3])
        return remote(sum_out.at[e, n], dst, sum_ss.at[e, n], sem, y_peer(SUM_STEPS[e][n]))

    def sum_send(e, n, value):
        sum_out[e, n] = value.astype(BF16)
        sum_copy(e, n).start()

    def sum_end(e):
        value = summed(e, 0)
        for n in (2, 3, 0, 1):
            remote(
                sum_out.at[e, n + 3], end_in.at[e, n], sum_ss.at[e, n + 3], end_rs.at[e, n], y_peer(1)
            ).wait_recv()
            value = value + end_in[e, n].astype(F32)
        return value

    def pair_sum(n):
        return remote(z_out.at[n], z_in.at[n], pair_ss.at[2 + n], pair_rs.at[2 + n], pairs[n])

    half_places = Y // 2
    lax.fori_loop(0, half_places, functools.partial(features, 1), 0)
    lax.fori_loop(0, 2, functools.partial(features, 0), 0)
    for m in range(half_places):
        sib_copy(1, m).wait_recv()
    for n, rel in ((0, 5), (1, 3), (3, 6), (4, 2), (5, 7), (6, 1)):
        sum_send(1, n, summed(1, rel))
    lax.fori_loop(2, half_places, functools.partial(features, 0), 0)
    for m in (0, 1):
        sib_copy(0, m).wait_recv()
    for n, rel in ((2, 4), (0, 5), (1, 3)):
        sum_send(0, n, summed(0, rel))
    for m in (2, 3):
        sib_copy(0, m).wait_recv()
    for n, rel in ((5, 7), (6, 1)):
        sum_send(0, n, summed(0, rel))
    z_out[1] = (summed(1, 4) + relay_wait(1, 0) + relay_wait(1, 1)).astype(BF16)
    pair_sum(1).start()
    z_out[0] = sum_end(1).astype(BF16)
    pair_sum(0).start()
    for n, rel in ((3, 6), (4, 2)):
        value = summed(0, rel) + relay_wait(0, n - 3)
        if n == 3:
            value = value + relay_wait(0, 2)
        sum_send(0, n, value)
    out_ref[...] = sum_end(0)

    for n in (0, 1):
        pair_copy(n).wait_send()
    for e in (0, 1):
        for n in range(len(AG_SENDS[e])):
            ag_send(e, n).wait_send()
        for n in SUM_SENDS[e]:
            sum_copy(e, n).wait_send()
        for rel in range(Y):
            ag_sib(e, rel).wait_send()
    for j in (1, 2, 3):
        kv_copy(kall, 0, j).wait_send()
        kv_copy(vall, 1, j).wait_send()
        dkv_copy(j).wait_send()

    def drain(i, carry):
        d = way(i)

        @pl.when(z_valid(d))
        def _():
            q_copy(d).wait_send()
            dq_copy(d).wait_send()
            for which in (0, 1):
                o_copy(which, d).wait_send()
                do_copy(which, d).wait_send()

        return carry

    lax.fori_loop(1, WAYS, drain, 0)

    for e in (0, 1):
        for m in range(half_places):
            sib_copy(e, m).wait_send()
    pair_sum(0).wait()
    pair_sum(1).wait()
    out_ref[...] += z_in[0].astype(F32) + z_in[1].astype(F32)


def on_device(
    grad_out, w_out, query_proj, key_proj, value_proj, w_query, w_key, w_value, tile_keys
):
    block = grad_out.shape[1]
    features = w_out.shape[1]
    dma = pltpu.SemaphoreType.DMA
    square = (TILE, TILE)
    column = (X * TILE, TILE)
    row = (1, TILE)
    stat = (WAYS, 8, TILE)
    piece = (block, TILE)
    anywhere = pl.BlockSpec(memory_space=pl.ANY)
    return pl.pallas_call(
        kernel,
        out_shape=jax.ShapeDtypeStruct(piece, F32),
        in_specs=[anywhere] * 8 + [pl.BlockSpec(memory_space=pltpu.SMEM)],
        out_specs=pl.BlockSpec(memory_space=pltpu.VMEM),
        scratch_shapes=[
            pltpu.VMEM((features, TILE), BF16),
            pltpu.VMEM(w_out.shape, BF16),
            pltpu.VMEM((WAYS, *square), BF16),
            pltpu.VMEM(column, BF16),
            pltpu.VMEM(column, BF16),
            pltpu.VMEM(column[::-1], BF16),
            pltpu.VMEM(column[::-1], BF16),
            pltpu.VMEM((features, 3 * TILE), BF16),
            pltpu.VMEM((WAYS, *column), F32),
            pltpu.VMEM(stat, F32),
            pltpu.VMEM((WAYS, *square), BF16),
            pltpu.VMEM(stat, F32),
            pltpu.VMEM((WAYS, *square), BF16),
            pltpu.VMEM(stat, F32),
            pltpu.VMEM(square, F32),
            pltpu.VMEM(row, F32),
            pltpu.VMEM(row, F32),
            pltpu.VMEM((WAYS, *square), BF16),
            pltpu.VMEM(stat, F32),
            pltpu.VMEM(column, F32),
            pltpu.VMEM(column, F32),
            pltpu.VMEM((WAYS, *square), BF16),
            pltpu.VMEM((WAYS, *square), BF16),
            pltpu.VMEM(square, F32),
            pltpu.VMEM((X, 2 * TILE, TILE), BF16),
            pltpu.VMEM((X, 2 * TILE, TILE), BF16),
            pltpu.VMEM((3 * TILE, TILE), BF16),
            pltpu.VMEM((2, Y // 2, 2, *piece), BF16),
            pltpu.VMEM((2, Y // 2, 2, *piece), BF16),
            pltpu.VMEM((2, Y // 2, 2, *piece), F32),
            pltpu.VMEM((2, 7, *piece), BF16),
            pltpu.VMEM((2, 3, *piece), BF16),
            pltpu.VMEM((2, 4, *piece), BF16),
            pltpu.VMEM((2, *piece), BF16),
            pltpu.VMEM((2, *piece), BF16),
            dma((8,)),
            dma((2, 7)), dma((2, Y)),
            dma((2, Y)), dma((2, Y)),
            dma((4,)), dma((4,)),
            dma((2, X)), dma((2, X)),
            dma((WAYS,)), dma((WAYS,)),
            dma((2, WAYS)), dma((2, WAYS)),
            dma((2, WAYS)), dma((2, WAYS)),
            dma((WAYS,)), dma((WAYS,)),
            dma((X,)), dma((X,)),
            dma((2, Y // 2)), dma((2, Y // 2)),
            dma((2, 7)), dma((2, 3)), dma((2, 4)),
        ],
        compiler_params=pltpu.CompilerParams(
            collective_id=0, has_side_effects=True, vmem_limit_bytes=60 * 1024 * 1024
        ),
    )(grad_out.T, w_out, query_proj, key_proj, value_proj, w_query, w_key, w_value, tile_keys.T)


def solution(mesh):
    return jax.shard_map(
        on_device,
        mesh=mesh,
        in_specs=(
            P("ctx", "tp"),
            P("tp", None),
            P("ctx", "tp"),
            P("ctx", "tp"),
            P("ctx", "tp"),
            P(None, "tp"),
            P(None, "tp"),
            P(None, "tp"),
            P(),
        ),
        out_specs=P("tp", "ctx"),
        check_vma=False,
    )
```
